32 devices in a mesh: row: 4 (over y, x), col: 8 (over z, core).
Axes of the slice: x: 2, y: 2, z: 4, core: 2. Of those that a mesh axis runs over, the one named last changes fastest.
Arguments:
- hidden: bfloat16 [5120, 5120], P('col'), may hold values from -26 to 26
- lengths: int32 [4], replicated, may hold values from 512 to 2048, as said below
- owner: int32 [4], replicated, may hold values from 0 to 7, as said below
- page_table: int32 [4, 16], replicated, may hold values from 0 to 15, as said below
- qkv_train: float32 [3, 5120, 3072], P(None, 'row', 'col'), may hold values from -1 to 1
- qk_gain: float32 [2, 3072], P(None, 'row'), may hold values from 0.1 to 1.9
- o_weight: bfloat16 [3072, 5120], P('row'), may hold values from -1.5 to 1.5
- post_gain: float32 [5120], P('row'), may hold values from 0.1 to 1.9
- gate_up_train: float32 [2, 5120, 13824], P(None, 'row', 'col'), may hold values from -0.078125 to 0.078125
Outputs:
- layer_out: bfloat16 [5120, 5120], P('col', 'row')
- kv_cache: bfloat16 [8, 16, 2, 128, 3072], P('col', None, None, None, 'row')
- qkv_server: bfloat16 [3, 4, 1280, 3072], P(None, None, 'col', 'row')
- gate_up_server: bfloat16 [2, 4, 1280, 13824], P(None, None, 'col', 'row')
The draws below stay inside these ranges and needn't reach their ends.
Inputs may be any that keep to these rules, and one draw needn't show every extreme that they name: The lengths add up to 5120; one prompt has 2048 tokens and one 512. `owner`: the owners are distinct. `page_table`: each row is a permutation of the 16 slots.
All inputs are finite; a program needn't handle non-finite values.
Results may differ from the reference program's by a relative error of at most 0.025.
Values may be sent and summed in bfloat16 or wider, within the bound.
No kernel may reach another device: no remote copies, remote signals or barrier semaphores. Data moves between devices by JAX's collectives and lax.ppermute only.
A program may use at most 256 MiB of HBM per device.

```python
import math
import jax
import jax.numpy as jnp
from jax import lax

D = 5120
HD = 128
FF = 13824
HEADS = 24
PROMPTS = 4
LMAX = 2048
LMIN = 512
PAGE = 128
PAGES = 16
TOKENS = 5120
N_ROW = 4
N_COL = 8


def draw_hidden(key, part):
    noise_key = jax.random.fold_in(key, 11)
    values = jnp.clip(jax.random.normal(noise_key, (TOKENS, D), jnp.float32), -6.0, 6.0)
    return values.astype(jnp.bfloat16)


def draw_qkv_train(key, part):
    heads_width = HEADS * HD
    columns = jnp.arange(heads_width, dtype=jnp.float32)
    column_scale = jnp.sqrt(3.0 ** (columns / heads_width))[None, None, :]
    base_draw = jnp.clip(jax.random.normal(jax.random.fold_in(key, 22), (3, D, heads_width), jnp.float32), -6.0, 6.0)
    values = base_draw * column_scale / math.sqrt(D)
    return values


def draw_o_weight(key, part):
    columns = jnp.arange(D, dtype=jnp.float32)
    column_scale = jnp.sqrt(3.0 ** (columns / D))[None, :] / math.sqrt(HEADS * HD)
    base_draw = jnp.clip(jax.random.normal(jax.random.fold_in(key, 32), (HEADS * HD, D), jnp.float32), -6.0, 6.0)
    return (base_draw * column_scale).astype(jnp.bfloat16)


def draw_lengths(key, part):
    middle = jax.random.randint(jax.random.fold_in(key, 41), (), LMIN, LMAX + 1).astype(jnp.int32)
    values = jnp.stack([jnp.int32(LMAX), jnp.int32(LMIN), middle, jnp.int32(LMAX + LMIN) - middle]).astype(jnp.int32)
    return values[jax.random.permutation(jax.random.fold_in(key, 42), PROMPTS)]


def draw_owner(key, part):
    middle = jax.random.permutation(jax.random.fold_in(key, 51), N_COL - 2)[:PROMPTS - 2] + 1
    values = jnp.concatenate([jnp.array([0, N_COL - 1], jnp.int32), middle.astype(jnp.int32)])
    return values[jax.random.permutation(jax.random.fold_in(key, 52), PROMPTS)]


def draw_page_table(key, part):
    row_keys = jax.random.split(jax.random.fold_in(key, 61), PROMPTS)
    return jax.vmap(lambda row_key: jax.random.permutation(row_key, PAGES))(row_keys).astype(jnp.int32)


def block_levels(key, extent, pieces, smallest, largest):
    gain = 1.0
    for axis_at, shards_of in pieces:
        steps = jax.random.uniform(jax.random.fold_in(jax.random.fold_in(key, 6), axis_at), (shards_of,), jnp.float32, smallest / len(pieces), largest / len(pieces))
        gain = gain * jnp.repeat(jnp.exp(steps), extent[axis_at] // shards_of).reshape((-1,) + (1,) * (len(extent) - 1 - axis_at))
    return gain


def normal_values(key, extent, scale, most, cuts=(), kind=jnp.bfloat16):
    result = jax.random.normal(key, extent, jnp.float32) * scale
    if len(cuts) > 0:
        result = block_levels(key, extent, cuts, -0.22, 0.18) * result
    return jnp.clip(result, min=-most, max=most).astype(kind)


def setup_inputs(seed: int = 0) -> dict:
    key_list = jax.random.split(jax.random.key(seed), 10)
    hidden = draw_hidden(jax.random.fold_in(key_list[9], 71), 0)
    lengths = draw_lengths(jax.random.fold_in(key_list[9], 71), 0)
    owner = draw_owner(jax.random.fold_in(key_list[9], 71), 0)
    page_table = draw_page_table(jax.random.fold_in(key_list[9], 71), 0)
    qkv_train = draw_qkv_train(jax.random.fold_in(key_list[9], 71), 0)
    qk_gain = jnp.clip(1.0 + 0.18 * jax.random.normal(key_list[5], (2, HEADS * HD), jnp.float32), 0.1, 1.9)
    o_weight = draw_o_weight(jax.random.fold_in(key_list[9], 71), 0)
    post_gain = jnp.clip(1.0 + 0.18 * jax.random.normal(key_list[7], (D,), jnp.float32), 0.1, 1.9)
    gate_up_train = normal_values(key_list[8], (2, D, FF), D ** -0.5, 0.078125, ((1, 4), (2, 8)), jnp.float32)
    return dict(hidden=hidden, lengths=lengths, owner=owner, page_table=page_table, qkv_train=qkv_train, qk_gain=qk_gain, o_weight=o_weight, post_gain=post_gain, gate_up_train=gate_up_train)


norm_epsilon = 1e-06
rope_theta = 500000.0
big_negative = -1e+30

def inverse_rms(squares, features):
    return lax.rsqrt(squares / features + norm_epsilon)

def rotate_heads(inputs, positions):
    half_dim = inputs.shape[-1] // 2
    frequency = rope_theta ** (-2.0 * jnp.arange(half_dim, dtype=jnp.float32) / inputs.shape[-1])
    angles = positions.astype(jnp.float32)[:, None] * frequency[None, :]
    cosine = jnp.cos(angles)[:, None, :]
    sine_part = jnp.sin(angles)[:, None, :]
    lower_half = inputs[..., :half_dim]
    upper_half = inputs[..., half_dim:]
    return jnp.concatenate([lower_half * cosine - upper_half * sine_part, upper_half * cosine + lower_half * sine_part], axis=-1)

def locate_tokens(token_index, lengths):
    prompt_ends = jnp.cumsum(lengths).astype(jnp.int32)
    prompt_starts = prompt_ends - lengths
    segment = lax.optimization_barrier(jnp.sum((token_index[:, None] >= prompt_ends[None, :]).astype(jnp.int32), axis=1))
    onehot = segment[:, None] == jnp.arange(lengths.shape[0], dtype=jnp.int32)[None, :]
    position = token_index - lax.optimization_barrier(jnp.sum(jnp.where(onehot, prompt_starts[None, :], 0), axis=1))
    return (segment, position)

def reference(hidden, lengths, owner, page_table, qkv_train, qk_gain, o_weight, post_gain, gate_up_train):
    heads_width = HEADS * HD
    row_width = D // N_ROW
    col_block = D // (N_ROW * N_COL)
    qkv_server = qkv_train.astype(jnp.bfloat16).reshape(3, N_ROW, row_width, heads_width)
    gate_up_server = gate_up_train.astype(jnp.bfloat16).reshape(2, N_ROW, row_width, FF)
    token_index = jnp.arange(TOKENS, dtype=jnp.int32)
    segment, position = locate_tokens(token_index, lengths)
    hidden_blocks = hidden.astype(jnp.float32).reshape(TOKENS, N_ROW, N_COL, col_block)
    weight_blocks = qkv_server.astype(jnp.float32).reshape(3, N_ROW, N_COL, col_block, heads_width)
    projected = jnp.zeros((3, TOKENS, heads_width), jnp.float32)
    for column in range(N_COL):
        block_product = jnp.einsum('trb,jrbh->jth', hidden_blocks[:, :, column], weight_blocks[:, :, column])
        projected = projected + lax.optimization_barrier(block_product.astype(jnp.bfloat16)).astype(jnp.float32)
    query_rows = projected[0]
    key_rows = projected[1]
    value_rows = projected[2]
    query_norm = query_rows * inverse_rms(lax.optimization_barrier(jnp.sum(query_rows * query_rows, axis=1)), heads_width)[:, None] * qk_gain[0]
    key_norm = key_rows * inverse_rms(lax.optimization_barrier(jnp.sum(key_rows * key_rows, axis=1)), heads_width)[:, None] * qk_gain[1]
    query_rot = rotate_heads(query_norm.reshape(TOKENS, HEADS, HD), position).astype(jnp.bfloat16)
    key_rot = rotate_heads(key_norm.reshape(TOKENS, HEADS, HD), position).astype(jnp.bfloat16)
    value_heads = value_rows.reshape(TOKENS, HEADS, HD).astype(jnp.bfloat16)
    allowed = (segment[:, None] == segment[None, :]) & (token_index[None, :] <= token_index[:, None])

    def one_head(operands):
        query_head, key_head, value_head = operands
        scores = jnp.dot(query_head, key_head.T, preferred_element_type=jnp.float32) / math.sqrt(HD)
        masked = jnp.where(allowed, scores, big_negative)
        row_max = lax.optimization_barrier(jnp.max(masked, axis=1, keepdims=True))
        exponent = jnp.where(allowed, jnp.exp(masked - row_max), 0.0)
        numerator = jnp.dot(exponent.astype(jnp.bfloat16), value_head, preferred_element_type=jnp.float32)
        return numerator / lax.optimization_barrier(jnp.sum(exponent, axis=1, keepdims=True))
    attention = lax.map(one_head, (query_rot.transpose(1, 0, 2), key_rot.transpose(1, 0, 2), value_heads.transpose(1, 0, 2)))
    attention = attention.transpose(1, 0, 2).reshape(TOKENS, heads_width).astype(jnp.bfloat16)
    heads_per_row = heads_width // N_ROW
    attention_out = jnp.zeros((TOKENS, D), jnp.float32)
    for group in range(N_ROW):
        lower = group * heads_per_row
        group_product = jnp.dot(attention[:, lower:lower + heads_per_row], o_weight[lower:lower + heads_per_row], preferred_element_type=jnp.float32)
        attention_out = attention_out + lax.optimization_barrier(group_product.astype(jnp.bfloat16)).astype(jnp.float32)
    normalized = attention_out * inverse_rms(lax.optimization_barrier(jnp.sum(attention_out * attention_out, axis=1)), D)[:, None] * post_gain
    layer_out = (hidden.astype(jnp.float32) + normalized).astype(jnp.bfloat16)
    stacked = jnp.stack([key_rot.reshape(TOKENS, heads_width), value_heads.reshape(TOKENS, heads_width)], axis=1)
    padded = jnp.concatenate([stacked, jnp.zeros((LMAX, 2, heads_width), jnp.bfloat16)], axis=0)
    prompt_ends = jnp.cumsum(lengths).astype(jnp.int32)
    prompt_starts = prompt_ends - lengths
    kv_cache = jnp.zeros((N_COL, PAGES, 2, PAGE, heads_width), jnp.bfloat16)
    for prompt in range(PROMPTS):
        window = lax.dynamic_slice_in_dim(padded, prompt_starts[prompt].astype(jnp.int32), LMAX, 0)
        inside = jnp.arange(LMAX, dtype=jnp.int32) < lengths[prompt]
        window = jnp.where(inside[:, None, None], window, jnp.zeros((), jnp.bfloat16))
        pages_data = window.reshape(PAGES, PAGE, 2, heads_width).transpose(0, 2, 1, 3)
        kv_cache = kv_cache.at[owner[prompt], page_table[prompt]].set(pages_data)
    return (layer_out, kv_cache, qkv_server, gate_up_server)
```

```python
import functools
import math

import jax
import jax.numpy as jnp
from jax import lax
from jax.experimental import pallas as pl
from jax.experimental.pallas import tpu as pltpu
from jax.sharding import PartitionSpec as P

HD = 128
PAGE = 128
PAGES = 16
BOTH = ("row", "col")

norm_epsilon = 1e-06
rope_theta = 500000.0
big_negative = -1e30


def inverse_rms(squares, features):
    return lax.rsqrt(squares / features + norm_epsilon)


def permute(x, n_row, n_col, target):
    pairs = []
    for r in range(n_row):
        for c in range(n_col):
            r2, c2 = target(r, c)
            pairs.append((r * n_col + c, r2 * n_col + c2))
    return lax.ppermute(x, BOTH, pairs)


def after(x, *others):
    return lax.optimization_barrier((x,) + others)[0]


def pick(x, index, axis=0):
    return lax.dynamic_index_in_dim(x, index, axis, keepdims=False)


class Grid:
    def __init__(self):
        self.n_row = lax.axis_size("row")
        self.n_col = lax.axis_size("col")
        self.planes = self.n_col // 2
        self.row = lax.axis_index("row")
        self.col = lax.axis_index("col")
        self.plane = self.col // 2
        self.core = self.col % 2

    def move(self, x, target):
        return permute(x, self.n_row, self.n_col, target)

    def other_core(self, x):
        return self.move(x, lambda r, c: (r, c ^ 1))

    def row_xor(self, x, i):
        return self.move(x, lambda r, c: (r ^ i, c))

    def gather_row(self, x):
        if self.n_row != 4:
            return [x] + [self.row_xor(x, i) for i in range(1, self.n_row)]
        half = x.shape[0] // 2
        first = self.row_xor(x, 1)
        second = self.row_xor(x, 2)
        third = jnp.concatenate(
            [self.row_xor(first[:half], 2), self.row_xor(second[half:], 1)], axis=0
        )
        return [x, first, second, third]

    def across(self, block, i):
        return self.move(block, lambda r, c: (r, (((c // 2) ^ i ^ r) * 2) + c % 2))

    def down(self, block, i):
        return self.move(block, lambda r, c: ((c // 2) ^ i ^ r, c))

    def join_cores(self, mine, other, axis):
        return jnp.where(
            self.core == 0,
            jnp.concatenate([mine, other], axis=axis),
            jnp.concatenate([other, mine], axis=axis),
        )


def attend_kernel(pieces, tokens, piece_tokens, heads, prompts, info, q_ref, *refs):
    kv_refs, out_ref = refs[:pieces], refs[pieces]
    block = pl.program_id(0)
    rows = q_ref.shape[1]
    width = heads * HD
    scale = math.log2(math.e) / math.sqrt(HD)
    first = block * tokens + info[prompts]
    first_start = jnp.int32(0)
    row_id = first + lax.broadcasted_iota(jnp.int32, (rows, 1), 0)
    row_start = jnp.zeros((rows, 1), jnp.int32)
    for p in range(prompts):
        end = info[p]
        first_start = jnp.where(end <= first, jnp.maximum(first_start, end), first_start)
        row_start = jnp.where(end <= row_id, jnp.maximum(row_start, end), row_start)
    lowest = first_start // tokens
    lane = lax.broadcasted_iota(jnp.int32, (1, tokens), 1)
    place = lane + info[prompts + 1]
    for i in range(1, pieces):
        place = jnp.where(
            lane >= i * piece_tokens, lane + (info[prompts + 1 + i] - i * piece_tokens), place
        )
    for head in range(heads):
        at = head * HD
        query = q_ref[0, :, at : at + HD]

        def step(chunk, state):
            top, total, acc = state
            keys = jnp.concatenate([ref[chunk, :, at : at + HD] for ref in kv_refs], axis=0)
            values = jnp.concatenate(
                [ref[chunk, :, width + at : width + at + HD] for ref in kv_refs], axis=0
            )
            scores = lax.dot_general(
                query, keys, (((1,), (1,)), ((), ())), preferred_element_type=jnp.float32
            )
            key_id = chunk * tokens + place
            allowed = (key_id <= row_id) & (key_id >= row_start)
            scores = jnp.where(allowed, scores, big_negative)
            new_top = jnp.maximum(top, jnp.max(scores, axis=1, keepdims=True))
            shrink = jnp.exp2((top - new_top) * scale)
            weights = jnp.exp2((scores - new_top) * scale)
            total = total * shrink + jnp.sum(weights, axis=1, keepdims=True)
            acc = acc * shrink + jnp.dot(
                weights.astype(jnp.bfloat16), values, preferred_element_type=jnp.float32
            )
            return new_top, total, acc

        state = (
            jnp.full((rows, 1), big_negative, jnp.float32),
            jnp.zeros((rows, 1), jnp.float32),
            jnp.zeros((rows, HD), jnp.float32),
        )
        top, total, acc = lax.fori_loop(lowest, block + 1, step, state)
        out_ref[0, :, at : at + HD] = (acc / total).astype(out_ref.dtype)


def attend(query, kv_pieces, info, tokens, prompts):
    blocks, rows, width = query.shape
    pieces = len(kv_pieces)
    piece_tokens = kv_pieces[0].shape[1]
    kernel = functools.partial(
        attend_kernel, pieces, tokens, piece_tokens, width // HD, prompts
    )
    return pl.pallas_call(
        kernel,
        grid_spec=pltpu.PrefetchScalarGridSpec(
            num_scalar_prefetch=1,
            grid=(blocks,),
            in_specs=[pl.BlockSpec((1, rows, width), lambda b, info: (b, 0, 0))]
            + [pl.BlockSpec(x.shape, lambda b, info: (0, 0, 0)) for x in kv_pieces],
            out_specs=pl.BlockSpec((1, rows, width), lambda b, info: (b, 0, 0)),
        ),
        out_shape=jax.ShapeDtypeStruct(query.shape, jnp.bfloat16),
        compiler_params=pltpu.CompilerParams(vmem_limit_bytes=48 * 1024 * 1024),
        cost_estimate=pl.CostEstimate(
            flops=4 * blocks * rows * width * tokens * 3,
            bytes_accessed=4 * blocks * rows * width + 2 * sum(x.size for x in kv_pieces),
            transcendentals=blocks * rows * (width // HD) * tokens * 3,
        ),
        name="attend",
    )(info, query, *kv_pieces)


def page_kernel(info, pages_ref, out_ref):
    page = info[pl.program_id(0)]
    row = page * PAGE + lax.broadcasted_iota(jnp.int32, (1, PAGE, 1), 1)
    inside = row < info[PAGES]
    out_ref[0] = jnp.where(inside, pages_ref[0].astype(jnp.float32), 0.0).astype(out_ref.dtype)


def place_pages(pages, info):
    shape = pages.shape
    spec = (1,) + shape[1:]
    return pl.pallas_call(
        page_kernel,
        grid_spec=pltpu.PrefetchScalarGridSpec(
            num_scalar_prefetch=1,
            grid=(PAGES,),
            in_specs=[pl.BlockSpec(spec, lambda s, info: (info[s], 0, 0, 0))],
            out_specs=pl.BlockSpec(spec, lambda s, info: (s, 0, 0, 0)),
        ),
        out_shape=jax.ShapeDtypeStruct(shape, pages.dtype),
        cost_estimate=pl.CostEstimate(
            flops=pages.size, bytes_accessed=4 * pages.size, transcendentals=0
        ),
        name="place_pages",
    )(info, pages)


def local(
    hidden, lengths, owner, page_table, qkv_train, qk_gain, o_weight, post_gain, gate_up_train
):
    grid = Grid()
    n_row, n_col, planes = grid.n_row, grid.n_col, grid.planes
    row, col, plane, core = grid.row, grid.col, grid.plane, grid.core
    bf16 = jnp.bfloat16
    prompts = lengths.shape[0]
    tokens, width = hidden.shape
    part = tokens // n_row
    row_width = width // n_row
    col_block = row_width // n_col
    units = qkv_train.shape[2]
    heads_width = units * n_col
    ff_units = gate_up_train.shape[2]

    prompt_ends = jnp.cumsum(lengths)
    prompt_starts = prompt_ends - lengths

    quarter = lax.dynamic_slice_in_dim(hidden, row * part, part, 0).reshape(part, n_row, row_width)
    quarter = jnp.concatenate([pick(quarter, row ^ i, 1) for i in range(n_row)], axis=1)
    gathered = lax.all_gather(quarter, "col", axis=0, tiled=True)
    weights = qkv_train.astype(bf16).transpose(1, 0, 2).reshape(row_width, 3 * units)
    weight_pieces = grid.gather_row(weights)
    gain = pick(lax.all_gather(qk_gain, "row", axis=0), plane)
    whole_heads = units % HD == 0
    held = units if whole_heads else 2 * units
    if whole_heads:
        gain = lax.dynamic_slice_in_dim(gain, core * units, units, 1)

    projected = 0.0
    for i in range(n_row):
        projected = projected + jnp.dot(
            gathered[:, i * row_width : (i + 1) * row_width],
            weight_pieces[i],
            preferred_element_type=jnp.float32,
        )
    rows_here = n_col * part
    projected = projected.reshape(rows_here, 3, units)
    squares = jnp.sum(projected[:, :2] * projected[:, :2], axis=2)
    squares = jnp.sum(lax.all_gather(squares.T, "col", axis=0), axis=0)
    inverse = inverse_rms(squares, heads_width)
    if not whole_heads:
        projected = grid.join_cores(projected, grid.other_core(projected), 2)

    token = (
        jnp.arange(n_col, dtype=jnp.int32)[:, None] * tokens
        + row * part
        + jnp.arange(part, dtype=jnp.int32)[None, :]
    ).reshape(rows_here)
    start = jnp.max(jnp.where(token[:, None] >= prompt_ends[None, :], prompt_ends[None, :], 0), axis=1)
    position = token - start
    half = HD // 2
    frequency = rope_theta ** (-2.0 * jnp.arange(half, dtype=jnp.float32) / HD)
    angles = position.astype(jnp.float32)[:, None] * frequency[None, :]
    cosine = jnp.cos(angles)
    sine = jnp.sin(angles)
    cosine = jnp.concatenate([cosine, cosine], axis=1)[:, None, :]
    sine = jnp.concatenate([-sine, sine], axis=1)[:, None, :]

    def rotate(x):
        x = x.reshape(rows_here, held // HD, HD)
        swapped = jnp.concatenate([x[..., half:], x[..., :half]], axis=-1)
        return (x * cosine + swapped * sine).reshape(rows_here, held).astype(bf16)

    query = rotate(projected[:, 0] * inverse[0][:, None] * gain[0])
    key = rotate(projected[:, 1] * inverse[1][:, None] * gain[1])
    value = projected[:, 2].astype(bf16)
    kv = jnp.concatenate([key, value], axis=1)

    kv_pieces = [x.reshape(n_col, part, 2 * held) for x in grid.gather_row(kv)]
    offsets = jnp.stack([(row ^ i) * part for i in range(n_row)])
    if part % 16:
        stacked = jnp.stack(kv_pieces)
        natural = jnp.stack([pick(stacked, row ^ r) for r in range(n_row)], axis=1)
        kv_pieces = [natural.reshape(n_col, tokens, 2 * held)]
        offsets = jnp.zeros((1,), jnp.int32)
    info = jnp.concatenate([prompt_ends, (row * part)[None], offsets]).astype(jnp.int32)
    attention = attend(query.reshape(n_col, part, held), kv_pieces, info, tokens, prompts)

    attention = attention.reshape(planes, 2, part, held)
    mine = pick(attention, core, 1)
    if whole_heads:
        attention = grid.join_cores(mine, grid.other_core(pick(attention, 1 - core, 1)), 2)
    else:
        attention = mine
    arrived = jnp.stack(
        [
            grid.down(grid.across(pick(attention, plane ^ i ^ row), i), i)
            for i in range(n_row)
        ]
    )
    attention_rows = jnp.concatenate(
        [pick(arrived, r ^ row ^ plane) for r in range(n_row)], axis=0
    )
    partial_out = jnp.dot(attention_rows, o_weight, preferred_element_type=jnp.float32).astype(bf16)
    partial_out = partial_out.reshape(tokens, n_row, row_width)
    summed = pick(partial_out, row, 1).astype(jnp.float32)
    for i in range(1, n_row):
        summed = summed + grid.row_xor(pick(partial_out, row ^ i, 1), i).astype(jnp.float32)
    out_squares = lax.psum(jnp.sum(summed * summed, axis=1), "row")
    normalized = summed * inverse_rms(out_squares, width)[:, None] * post_gain
    residual = lax.dynamic_slice_in_dim(hidden, row * row_width, row_width, 1).astype(jnp.float32)
    layer_out = (residual + normalized).astype(bf16)

    if not whole_heads:
        kv = jnp.concatenate(
            [lax.dynamic_slice_in_dim(x, core * units, units, 1) for x in (key, value)], axis=1
        )
    same_core = [list(range(k, n_col, 2)) for k in range(2)]
    kv_planes = lax.all_gather(kv, "col", axis=0, axis_index_groups=same_core)
    cache_pieces = [pick(kv_planes, row)] + [
        grid.row_xor(pick(kv_planes, row ^ i), i) for i in range(1, n_row)
    ]
    stacked = jnp.stack(cache_pieces).reshape(n_row, n_col, part, 2 * units)
    natural = jnp.stack([pick(stacked, row ^ r) for r in range(n_row)], axis=1)
    natural = natural.reshape(n_col * tokens, 2 * units)
    most = PAGES * PAGE
    natural = jnp.concatenate([natural, jnp.zeros((most, 2 * units), bf16)], axis=0)

    def start_of(owner_col):
        return jnp.sum(jnp.where(owner == owner_col, prompt_starts, 0))

    window_other = grid.other_core(
        lax.dynamic_slice_in_dim(natural, start_of(col ^ 1), most, 0)
    )
    window = lax.dynamic_slice_in_dim(natural, start_of(col), most, 0)
    pages = grid.join_cores(
        window.reshape(PAGES, PAGE, 2, units), window_other.reshape(PAGES, PAGE, 2, units), 3
    ).transpose(0, 2, 1, 3)
    mine = owner == col
    my_length = jnp.sum(jnp.where(mine, lengths, 0))
    my_table = jnp.sum(jnp.where(mine[:, None], page_table, 0), axis=0)
    page_index = jnp.arange(PAGES, dtype=jnp.int32)
    page_of_slot = jnp.sum(
        jnp.where(my_table[None, :] == page_index[:, None], page_index[None, :], 0), axis=1
    )
    page_of_slot = jnp.where(jnp.any(mine), page_of_slot, 0)
    cache = place_pages(pages, jnp.concatenate([page_of_slot, my_length[None]]).astype(jnp.int32))

    def swap_cores(blocks):
        other = grid.other_core(pick(blocks, 1 - core, 1))
        return pick(blocks, core, 1), other

    qkv_mine, qkv_other = swap_cores(weights.reshape(planes, 2, col_block, 3, units))
    qkv_blocks = grid.join_cores(qkv_mine, qkv_other, 3).reshape(planes, col_block, 6 * units)
    ff = gate_up_train.astype(bf16).reshape(2, planes, 2, col_block, ff_units)
    ff_blocks = [grid.join_cores(*swap_cores(ff[j]), 2) for j in range(2)]

    split = 2 if (col_block // 2) % 16 == 0 else 1
    step_rows = col_block // split
    chunks = [(b, s * step_rows) for b in ff_blocks for s in range(split)]
    chunks.append((qkv_blocks, None))
    results = []
    gate = gathered
    for blocks, at in chunks:
        sent = []
        for i in range(n_row):
            block = pick(blocks, plane ^ i ^ row)
            if at is not None:
                block = block[at : at + step_rows]
            sent.append(grid.across(after(block, gate), i))
        gate = sent[0][:8, :128]
        results.append(
            jnp.stack([grid.down(x, i) for i, x in enumerate(sent)])
        )

    def in_order(rounds):
        return jnp.stack([pick(rounds, r ^ row ^ plane) for r in range(n_row)])

    qkv_server = in_order(results[-1]).reshape(n_row, col_block, 3, 2 * units).transpose(2, 0, 1, 3)
    ff_server = [
        jnp.concatenate([in_order(x) for x in results[j * split : (j + 1) * split]], axis=1)
        for j in range(2)
    ]
    return (layer_out, cache[None], qkv_server, jnp.stack(ff_server))


def solution(mesh):
    in_specs = (
        P("col", None),
        P(),
        P(),
        P(),
        P(None, "row", "col"),
        P(None, "row"),
        P("row", None),
        P("row"),
        P(None, "row", "col"),
    )
    out_specs = (
        P("col", "row"),
        P("col", None, None, None, "row"),
        P(None, None, "col", "row"),
        P(None, None, "col", "row"),
    )
    return jax.shard_map(local, mesh=mesh, in_specs=in_specs, out_specs=out_specs, check_vma=False)
```

```python
import functools
import math

import jax
import jax.numpy as jnp
from jax import lax
from jax.experimental import pallas as pl
from jax.experimental.pallas import tpu as pltpu
from jax.sharding import PartitionSpec as P

HD = 128
PAGE = 128
PAGES = 16
BOTH = ("row", "col")

norm_epsilon = 1e-06
rope_theta = 500000.0
big_negative = -1e30


def inverse_rms(squares, features):
    return lax.rsqrt(squares / features + norm_epsilon)


def permute(x, n_row, n_col, target):
    pairs = []
    for r in range(n_row):
        for c in range(n_col):
            r2, c2 = target(r, c)
            pairs.append((r * n_col + c, r2 * n_col + c2))
    return lax.ppermute(x, BOTH, pairs)


def together(*values):
    return lax.optimization_barrier(values)


def pick(x, index, axis=0):
    return lax.dynamic_index_in_dim(x, index, axis, keepdims=False)


class Grid:
    def __init__(self):
        self.n_row = lax.axis_size("row")
        self.n_col = lax.axis_size("col")
        self.planes = self.n_col // 2
        self.row = lax.axis_index("row")
        self.col = lax.axis_index("col")
        self.plane = self.col // 2
        self.core = self.col % 2

    def move(self, x, target):
        return permute(x, self.n_row, self.n_col, target)

    def other_core(self, x):
        return self.move(x, lambda r, c: (r, c ^ 1))

    def row_xor(self, x, i):
        return self.move(x, lambda r, c: (r ^ i, c))

    def gather_row(self, x):
        if self.n_row != 4:
            return [x] + [self.row_xor(x, i) for i in range(1, self.n_row)]
        half = x.shape[0] // 2
        first = self.row_xor(x, 1)
        second = self.row_xor(x, 2)
        third = jnp.concatenate(
            [self.row_xor(first[:half], 2), self.row_xor(second[half:], 1)], axis=0
        )
        return [x, first, second, third]

    def over_planes(self, blocks):
        groups = [list(range(k, self.n_col, 2)) for k in range(2)]
        return lax.all_to_all(
            blocks, "col", split_axis=0, concat_axis=0, tiled=True, axis_index_groups=groups
        )

    def over_rows(self, blocks):
        moved = [pick(blocks, self.row)]
        for i in range(1, self.n_row):
            moved.append(self.row_xor(pick(blocks, self.row ^ i), i))
        return self.in_order(moved)

    def in_order(self, moved):
        stacked = jnp.stack(moved)
        return [pick(stacked, r ^ self.row) for r in range(self.n_row)]

    def join_cores(self, mine, other, axis):
        return jnp.where(
            self.core == 0,
            jnp.concatenate([mine, other], axis=axis),
            jnp.concatenate([other, mine], axis=axis),
        )


def attend_kernel(pieces, tokens, piece_tokens, heads, prompts, info, q_ref, *refs):
    kv_refs, out_ref = refs[:pieces], refs[pieces]
    block = pl.program_id(0)
    rows = q_ref.shape[1]
    width = heads * HD
    scale = math.log2(math.e) / math.sqrt(HD)
    first = block * tokens + info[prompts]
    first_start = jnp.int32(0)
    row_id = first + lax.broadcasted_iota(jnp.int32, (rows, 1), 0)
    row_start = jnp.zeros((rows, 1), jnp.int32)
    for p in range(prompts):
        end = info[p]
        first_start = jnp.where(end <= first, jnp.maximum(first_start, end), first_start)
        row_start = jnp.where(end <= row_id, jnp.maximum(row_start, end), row_start)
    lowest = first_start // tokens
    lane = lax.broadcasted_iota(jnp.int32, (1, tokens), 1)
    place = lane + info[prompts + 1]
    for i in range(1, pieces):
        place = jnp.where(
            lane >= i * piece_tokens, lane + (info[prompts + 1 + i] - i * piece_tokens), place
        )
    for head in range(heads):
        at = head * HD
        query = q_ref[0, :, at : at + HD]

        def step(chunk, state):
            top, total, acc = state
            keys = jnp.concatenate([ref[chunk, :, at : at + HD] for ref in kv_refs], axis=0)
            values = jnp.concatenate(
                [ref[chunk, :, width + at : width + at + HD] for ref in kv_refs], axis=0
            )
            scores = lax.dot_general(
                query, keys, (((1,), (1,)), ((), ())), preferred_element_type=jnp.float32
            )
            key_id = chunk * tokens + place
            allowed = (key_id <= row_id) & (key_id >= row_start)
            scores = jnp.where(allowed, scores, big_negative)
            new_top = jnp.maximum(top, jnp.max(scores, axis=1, keepdims=True))
            shrink = jnp.exp2((top - new_top) * scale)
            weights = jnp.exp2((scores - new_top) * scale)
            total = total * shrink + jnp.sum(weights, axis=1, keepdims=True)
            acc = acc * shrink + jnp.dot(
                weights.astype(jnp.bfloat16), values, preferred_element_type=jnp.float32
            )
            return new_top, total, acc

        state = (
            jnp.full((rows, 1), big_negative, jnp.float32),
            jnp.zeros((rows, 1), jnp.float32),
            jnp.zeros((rows, HD), jnp.float32),
        )
        top, total, acc = lax.fori_loop(lowest, block + 1, step, state)
        out_ref[0, :, at : at + HD] = (acc / total).astype(out_ref.dtype)


def attend(query, kv_pieces, info, tokens, prompts):
    blocks, rows, width = query.shape
    pieces = len(kv_pieces)
    piece_tokens = kv_pieces[0].shape[1]
    kernel = functools.partial(
        attend_kernel, pieces, tokens, piece_tokens, width // HD, prompts
    )
    return pl.pallas_call(
        kernel,
        grid_spec=pltpu.PrefetchScalarGridSpec(
            num_scalar_prefetch=1,
            grid=(blocks,),
            in_specs=[pl.BlockSpec((1, rows, width), lambda b, info: (b, 0, 0))]
            + [pl.BlockSpec(x.shape, lambda b, info: (0, 0, 0)) for x in kv_pieces],
            out_specs=pl.BlockSpec((1, rows, width), lambda b, info: (b, 0, 0)),
        ),
        out_shape=jax.ShapeDtypeStruct(query.shape, jnp.bfloat16),
        compiler_params=pltpu.CompilerParams(vmem_limit_bytes=48 * 1024 * 1024),
        cost_estimate=pl.CostEstimate(
            flops=4 * blocks * rows * width * tokens * 3,
            bytes_accessed=4 * blocks * rows * width + 2 * sum(x.size for x in kv_pieces),
            transcendentals=blocks * rows * (width // HD) * tokens * 3,
        ),
        name="attend",
    )(info, query, *kv_pieces)


def turn_kernel(width, x_ref, scale_ref, angle_ref, gain_ref, query_ref, kv_ref):
    cosine = angle_ref[:, :HD]
    sine = angle_ref[:, HD:]
    for j, (out_ref, base) in enumerate(((query_ref, 0), (kv_ref, 0))):
        scale = scale_ref[:, j : j + 1]
        for at in range(0, width, HD):
            x = x_ref[:, j * width + at : j * width + at + HD]
            x = x * scale * gain_ref[j : j + 1, at : at + HD]
            turned = x * cosine + pltpu.roll(x, HD // 2, 1) * sine
            out_ref[:, at : at + HD] = turned.astype(out_ref.dtype)
    kv_ref[:, width:] = x_ref[:, 2 * width :].astype(kv_ref.dtype)


def turn(projected, scales, angles, gain):
    rows, width = projected.shape[0], projected.shape[1] // 3
    step = 160 if rows % 160 == 0 else rows
    return pl.pallas_call(
        functools.partial(turn_kernel, width),
        grid=(rows // step,),
        in_specs=[
            pl.BlockSpec((step, 3 * width), lambda b: (b, 0)),
            pl.BlockSpec((step, 2), lambda b: (b, 0)),
            pl.BlockSpec((step, 2 * HD), lambda b: (b, 0)),
            pl.BlockSpec((2, width), lambda b: (0, 0)),
        ],
        out_specs=[
            pl.BlockSpec((step, width), lambda b: (b, 0)),
            pl.BlockSpec((step, 2 * width), lambda b: (b, 0)),
        ],
        out_shape=[
            jax.ShapeDtypeStruct((rows, width), jnp.bfloat16),
            jax.ShapeDtypeStruct((rows, 2 * width), jnp.bfloat16),
        ],
        cost_estimate=pl.CostEstimate(
            flops=10 * rows * width, bytes_accessed=18 * rows * width, transcendentals=0
        ),
        name="turn",
    )(projected, scales, angles, gain)


def page_kernel(info, key_ref, value_ref, out_ref):
    page = info[pl.program_id(0)]
    row = page * PAGE + lax.broadcasted_iota(jnp.int32, (PAGE, 1), 0)
    inside = row < info[PAGES]
    for j, ref in enumerate((key_ref, value_ref)):
        kept = jnp.where(inside, ref[...].astype(jnp.float32), 0.0)
        out_ref[0, j] = kept.astype(out_ref.dtype)


def place_pages(keys, values, info):
    width = keys.shape[1]
    spec = pl.BlockSpec((PAGE, width), lambda s, info: (info[s], 0))
    return pl.pallas_call(
        page_kernel,
        grid_spec=pltpu.PrefetchScalarGridSpec(
            num_scalar_prefetch=1,
            grid=(PAGES,),
            in_specs=[spec, spec],
            out_specs=pl.BlockSpec((1, 2, PAGE, width), lambda s, info: (s, 0, 0, 0)),
        ),
        out_shape=jax.ShapeDtypeStruct((PAGES, 2, PAGE, width), keys.dtype),
        cost_estimate=pl.CostEstimate(
            flops=2 * keys.size, bytes_accessed=8 * keys.size, transcendentals=0
        ),
        name="place_pages",
    )(info, keys, values)


def local(
    hidden, lengths, owner, page_table, qkv_train, qk_gain, o_weight, post_gain, gate_up_train
):
    grid = Grid()
    n_row, n_col, planes = grid.n_row, grid.n_col, grid.planes
    row, col, plane, core = grid.row, grid.col, grid.plane, grid.core
    bf16 = jnp.bfloat16
    prompts = lengths.shape[0]
    tokens, width = hidden.shape
    part = tokens // n_row
    row_width = width // n_row
    col_block = row_width // n_col
    units = qkv_train.shape[2]
    heads_width = units * n_col
    ff_units = gate_up_train.shape[2]

    prompt_ends = jnp.cumsum(lengths)
    prompt_starts = prompt_ends - lengths

    quarter = lax.dynamic_slice_in_dim(hidden, row * part, part, 0).reshape(part, n_row, row_width)
    quarter = jnp.concatenate([pick(quarter, row ^ i, 1) for i in range(n_row)], axis=1)
    gathered = lax.all_gather(quarter, "col", axis=0, tiled=True)
    gain = lax.all_gather(qk_gain, "row", axis=0)
    weights = qkv_train.astype(bf16).transpose(1, 0, 2).reshape(row_width, 3 * units)
    weights, gain = together(weights, gain)
    gain = pick(gain, plane)
    weight_pieces = grid.gather_row(weights)

    def swap_cores(blocks, axis):
        other = grid.other_core(pick(blocks, 1 - core, axis))
        return pick(blocks, core, axis), other

    qkv_blocks = grid.join_cores(
        *swap_cores(weights.reshape(planes, 2, col_block, 3, units), 1), 3
    ).reshape(planes, col_block, 6 * units)
    ff = gate_up_train.astype(bf16).reshape(2, planes, 2, col_block, ff_units)
    ff_blocks = grid.join_cores(*swap_cores(ff, 2), 3)
    split = 2 if (col_block // 2) % 16 == 0 else 1
    step_rows = col_block // split
    chunks = [
        ff_blocks[j, :, s * step_rows : (s + 1) * step_rows]
        for j in range(2)
        for s in range(split)
    ]
    at_planes = [grid.over_planes(chunks[0])]

    head_rows = o_weight.shape[0] // 2
    half_rows = lax.dynamic_slice_in_dim(o_weight, core * head_rows, head_rows, 0)
    columns = [
        lax.dynamic_slice_in_dim(half_rows, (row ^ i) * row_width, row_width, 1)
        for i in range(n_row)
    ]
    all_weights, *columns = together(jnp.concatenate(weight_pieces, axis=0), *columns)
    columns = [columns[0]] + [grid.row_xor(columns[i], i) for i in range(1, n_row)]
    gathered, at_planes[0], qkv_blocks = together(gathered, at_planes[0], qkv_blocks)
    at_planes_qkv = grid.over_planes(qkv_blocks)
    at_rows = [grid.over_rows(at_planes[0])]
    whole_heads = units % HD == 0
    held = units if whole_heads else 2 * units
    if whole_heads:
        gain = lax.dynamic_slice_in_dim(gain, core * units, units, 1)

    projected = jnp.dot(gathered, all_weights, preferred_element_type=jnp.float32)
    rows_here = n_col * part
    squares = jnp.stack(
        [
            jnp.sum(jnp.square(projected[:, j * units : (j + 1) * units]), axis=1)
            for j in range(2)
        ]
    )
    squares = jnp.sum(lax.all_gather(squares, "col", axis=0), axis=0)
    inverse = inverse_rms(squares, heads_width).T
    if not whole_heads:
        projected = projected.reshape(rows_here, 3, units)
        projected = grid.join_cores(projected, grid.other_core(projected), 2)
        projected = projected.reshape(rows_here, 3 * held)

    token = (
        jnp.arange(n_col, dtype=jnp.int32)[:, None] * tokens
        + row * part
        + jnp.arange(part, dtype=jnp.int32)[None, :]
    ).reshape(rows_here)
    start = jnp.max(jnp.where(token[:, None] >= prompt_ends[None, :], prompt_ends[None, :], 0), axis=1)
    position = token - start
    half = HD // 2
    frequency = rope_theta ** (-2.0 * jnp.arange(half, dtype=jnp.float32) / HD)
    turns = position.astype(jnp.float32)[:, None] * frequency[None, :]
    cosine, sine = jnp.cos(turns), jnp.sin(turns)
    angles = jnp.concatenate([cosine, cosine, -sine, sine], axis=1)
    query, kv = turn(projected, inverse, angles, gain)

    query, kv, at_planes_qkv, chunks[1], at_rows[0], columns = together(
        query, kv, at_planes_qkv, chunks[1], at_rows[0], columns
    )
    columns = jnp.stack(columns)
    columns_other = grid.other_core(columns)
    at_planes.append(grid.over_planes(chunks[1]))
    key_or_value = [
        lax.dynamic_slice_in_dim(kv, j * held + core * units, units, 1)
        if not whole_heads
        else kv[:, j * units : (j + 1) * units]
        for j in range(2)
    ]
    same_core = [list(range(k, n_col, 2)) for k in range(2)]
    key_planes, value_planes = [
        lax.all_gather(x, "col", axis=0, axis_index_groups=same_core) for x in key_or_value
    ]

    kv_pieces = [x.reshape(n_col, part, 2 * held) for x in grid.gather_row(kv)]
    offsets = jnp.stack([(row ^ i) * part for i in range(n_row)])
    if part % 16:
        stacked = jnp.stack(kv_pieces)
        natural = jnp.stack([pick(stacked, row ^ r) for r in range(n_row)], axis=1)
        kv_pieces = [natural.reshape(n_col, tokens, 2 * held)]
        offsets = jnp.zeros((1,), jnp.int32)
    info = jnp.concatenate([prompt_ends, (row * part)[None], offsets]).astype(jnp.int32)
    kv_pieces[-1], at_planes_qkv = together(kv_pieces[-1], at_planes_qkv)
    at_rows_qkv = grid.over_rows(at_planes_qkv)
    attention = attend(query.reshape(n_col, part, held), kv_pieces, info, tokens, prompts)

    attention, at_planes[1], key_planes, at_rows_qkv, columns_other = together(
        attention, at_planes[1], key_planes, at_rows_qkv, columns_other
    )
    at_rows.append(grid.over_rows(at_planes[1]))
    key_rows = lax.all_to_all(key_planes, "row", split_axis=0, concat_axis=0, tiled=True)

    def place_rows(whole, first, parts):
        for at, blocks in enumerate(parts, first):
            j, s = divmod(at, split)
            whole = lax.dynamic_update_slice(
                whole, jnp.stack(blocks)[None], (j, 0, s * step_rows, 0)
            )
        return whole

    attention = attention.reshape(planes, 2, part, held)
    mine = pick(attention, core, 1)
    if whole_heads:
        attention = grid.join_cores(mine, grid.other_core(pick(attention, 1 - core, 1)), 2)
    else:
        attention = mine
    arrived = jnp.stack(
        [pick(attention, plane)]
        + [
            grid.move(pick(attention, plane ^ i), lambda r, c: (r, c ^ (2 * i)))
            for i in range(1, planes)
        ]
    )
    arrived, key_rows, chunks[2:3], at_rows[1], value_planes = together(
        arrived, key_rows, chunks[2:3], at_rows[1], value_planes
    )
    at_planes += [grid.over_planes(chunk) for chunk in chunks[2:3]]
    o_columns = jnp.concatenate(
        [
            grid.join_cores(pick(columns, row ^ r), pick(columns_other, row ^ r), 0)
            for r in range(n_row)
        ],
        axis=0,
    )
    ff_server = jnp.zeros((2, n_row, col_block, 2 * ff_units), bf16)
    ff_server = place_rows(ff_server, 0, at_rows)
    attention = jnp.concatenate([pick(arrived, h ^ plane) for h in range(planes)], axis=1)
    attention_rows = jnp.concatenate(grid.in_order(grid.gather_row(attention)), axis=0)
    attention_rows, at_planes[2:], chunks[3:] = together(
        attention_rows, at_planes[2:], chunks[3:]
    )
    at_rows += [grid.over_rows(blocks) for blocks in at_planes[2:]]
    at_planes += [grid.over_planes(chunk) for chunk in chunks[3:]]
    value_rows = jnp.stack(grid.over_rows(value_planes))
    summed = jnp.dot(attention_rows, o_columns, preferred_element_type=jnp.float32)
    out_squares = lax.psum(jnp.sum(summed * summed, axis=1), "row")
    normalized = summed * inverse_rms(out_squares, width)[:, None] * post_gain
    residual = lax.dynamic_slice_in_dim(hidden, row * row_width, row_width, 1).astype(jnp.float32)
    layer_out = (residual + normalized).astype(bf16)
    ff_server = place_rows(ff_server, 2, at_rows[2:])
    layer_out, at_planes[3:], ff_server = together(layer_out, at_planes[3:], ff_server)
    at_rows += [grid.over_rows(blocks) for blocks in at_planes[3:]]
    ff_server = place_rows(ff_server, 3, at_rows[3:])

    most = PAGES * PAGE

    def start_of(owner_col):
        return jnp.sum(jnp.where(owner == owner_col, prompt_starts, 0))

    def window(rows):
        rows = rows.reshape(n_row, n_col, part, units).transpose(1, 0, 2, 3)
        rows = rows.reshape(n_col * tokens, units)
        rows = jnp.concatenate([rows, jnp.zeros((most, units), bf16)], axis=0)
        other = grid.other_core(lax.dynamic_slice_in_dim(rows, start_of(col ^ 1), most, 0))
        return grid.join_cores(
            lax.dynamic_slice_in_dim(rows, start_of(col), most, 0), other, 1
        )

    mine = owner == col
    my_length = jnp.sum(jnp.where(mine, lengths, 0))
    my_table = jnp.sum(jnp.where(mine[:, None], page_table, 0), axis=0)
    page_index = jnp.arange(PAGES, dtype=jnp.int32)
    page_of_slot = jnp.sum(
        jnp.where(my_table[None, :] == page_index[:, None], page_index[None, :], 0), axis=1
    )
    page_of_slot = jnp.where(jnp.any(mine), page_of_slot, 0)
    cache = place_pages(
        window(key_rows),
        window(value_rows),
        jnp.concatenate([page_of_slot, my_length[None]]).astype(jnp.int32),
    )

    qkv_server = jnp.stack(at_rows_qkv).reshape(n_row, col_block, 3, 2 * units).transpose(2, 0, 1, 3)
    return (layer_out, cache[None], qkv_server, ff_server)


def solution(mesh):
    in_specs = (
        P("col", None),
        P(),
        P(),
        P(),
        P(None, "row", "col"),
        P(None, "row"),
        P("row", None),
        P("row"),
        P(None, "row", "col"),
    )
    out_specs = (
        P("col", "row"),
        P("col", None, None, None, "row"),
        P(None, None, "col", "row"),
        P(None, None, "col", "row"),
    )
    return jax.shard_map(local, mesh=mesh, in_specs=in_specs, out_specs=out_specs, check_vma=False)
```

```python
import functools
import math

import jax
import jax.numpy as jnp
from jax import lax
from jax.experimental import pallas as pl
from jax.experimental.pallas import tpu as pltpu
from jax.sharding import PartitionSpec as P

HD = 128
PAGE = 128
PAGES = 16
BOTH = ("row", "col")

norm_epsilon = 1e-06
rope_theta = 500000.0
big_negative = -1e30


def inverse_rms(squares, features):
    return lax.rsqrt(squares / features + norm_epsilon)


def permute(x, n_row, n_col, target):
    pairs = []
    for r in range(n_row):
        for c in range(n_col):
            r2, c2 = target(r, c)
            pairs.append((r * n_col + c, r2 * n_col + c2))
    return lax.ppermute(x, BOTH, pairs)


def together(*values):
    return lax.optimization_barrier(values)


def pick(x, index, axis=0):
    return lax.dynamic_index_in_dim(x, index, axis, keepdims=False)


def halves(x, rows, width):
    upper = lax.reduce_precision(x, 8, 7)
    pairs = jnp.stack([upper, x - upper]).astype(jnp.bfloat16).reshape(-1)
    return jnp.pad(pairs, (0, rows * width - pairs.size)).reshape(rows, width)


def unhalved(pairs, shape):
    count = 2 * math.prod(shape)
    pairs = pairs.reshape(-1)[:count].astype(jnp.float32)
    return jnp.sum(pairs.reshape((2,) + tuple(shape)), axis=0)


class Grid:
    def __init__(self):
        self.n_row = lax.axis_size("row")
        self.n_col = lax.axis_size("col")
        self.planes = self.n_col // 2
        self.row = lax.axis_index("row")
        self.col = lax.axis_index("col")
        self.plane = self.col // 2
        self.core = self.col % 2

    def move(self, x, target):
        return permute(x, self.n_row, self.n_col, target)

    def other_core(self, x):
        return self.move(x, lambda r, c: (r, c ^ 1))

    def row_xor(self, x, i):
        return self.move(x, lambda r, c: (r ^ i, c))

    def gather_row(self, x):
        if self.n_row != 4:
            return [x] + [self.row_xor(x, i) for i in range(1, self.n_row)]
        half = x.shape[0] // 2
        first = self.row_xor(x, 1)
        second = self.row_xor(x, 2)
        third = jnp.concatenate(
            [self.row_xor(first[:half], 2), self.row_xor(second[half:], 1)], axis=0
        )
        return [x, first, second, third]

    def over_planes(self, blocks):
        groups = [list(range(k, self.n_col, 2)) for k in range(2)]
        return lax.all_to_all(
            blocks, "col", split_axis=0, concat_axis=0, tiled=True, axis_index_groups=groups
        )

    def over_rows(self, blocks):
        moved = [pick(blocks, self.row)]
        for i in range(1, self.n_row):
            moved.append(self.row_xor(pick(blocks, self.row ^ i), i))
        return self.in_order(moved)

    def in_order(self, moved):
        stacked = jnp.stack(moved)
        return [pick(stacked, r ^ self.row) for r in range(self.n_row)]

    def join_cores(self, mine, other, axis):
        return jnp.where(
            self.core == 0,
            jnp.concatenate([mine, other], axis=axis),
            jnp.concatenate([other, mine], axis=axis),
        )


def attend_kernel(pieces, tokens, piece_tokens, heads, prompts, info, q_ref, *refs):
    kv_refs, out_ref = refs[:pieces], refs[pieces]
    block = pl.program_id(0)
    rows = q_ref.shape[1]
    width = heads * HD
    scale = math.log2(math.e) / math.sqrt(HD)
    first = block * tokens + info[prompts]
    first_start = jnp.int32(0)
    row_id = first + lax.broadcasted_iota(jnp.int32, (rows, 1), 0)
    row_start = jnp.zeros((rows, 1), jnp.int32)
    for p in range(prompts):
        end = info[p]
        first_start = jnp.where(end <= first, jnp.maximum(first_start, end), first_start)
        row_start = jnp.where(end <= row_id, jnp.maximum(row_start, end), row_start)
    lowest = first_start // tokens
    lane = lax.broadcasted_iota(jnp.int32, (1, tokens), 1)
    place = lane + info[prompts + 1]
    for i in range(1, pieces):
        place = jnp.where(
            lane >= i * piece_tokens, lane + (info[prompts + 1 + i] - i * piece_tokens), place
        )
    for head in range(heads):
        at = head * HD
        query = q_ref[0, :, at : at + HD]

        def step(chunk, state):
            top, total, acc = state
            keys = jnp.concatenate([ref[chunk, :, at : at + HD] for ref in kv_refs], axis=0)
            values = jnp.concatenate(
                [ref[chunk, :, width + at : width + at + HD] for ref in kv_refs], axis=0
            )
            scores = lax.dot_general(
                query, keys, (((1,), (1,)), ((), ())), preferred_element_type=jnp.float32
            )
            key_id = chunk * tokens + place
            allowed = (key_id <= row_id) & (key_id >= row_start)
            scores = jnp.where(allowed, scores, big_negative)
            new_top = jnp.maximum(top, jnp.max(scores, axis=1, keepdims=True))
            shrink = jnp.exp2((top - new_top) * scale)
            weights = jnp.exp2((scores - new_top) * scale)
            total = total * shrink + jnp.sum(weights, axis=1, keepdims=True)
            acc = acc * shrink + jnp.dot(
                weights.astype(jnp.bfloat16), values, preferred_element_type=jnp.float32
            )
            return new_top, total, acc

        state = (
            jnp.full((rows, 1), big_negative, jnp.float32),
            jnp.zeros((rows, 1), jnp.float32),
            jnp.zeros((rows, HD), jnp.float32),
        )
        top, total, acc = lax.fori_loop(lowest, block + 1, step, state)
        out_ref[0, :, at : at + HD] = (acc / total).astype(out_ref.dtype)


def attend(query, kv_pieces, info, tokens, prompts):
    blocks, rows, width = query.shape
    pieces = len(kv_pieces)
    piece_tokens = kv_pieces[0].shape[1]
    kernel = functools.partial(
        attend_kernel, pieces, tokens, piece_tokens, width // HD, prompts
    )
    return pl.pallas_call(
        kernel,
        grid_spec=pltpu.PrefetchScalarGridSpec(
            num_scalar_prefetch=1,
            grid=(blocks,),
            in_specs=[pl.BlockSpec((1, rows, width), lambda b, info: (b, 0, 0))]
            + [pl.BlockSpec(x.shape, lambda b, info: (0, 0, 0)) for x in kv_pieces],
            out_specs=pl.BlockSpec((1, rows, width), lambda b, info: (b, 0, 0)),
        ),
        out_shape=jax.ShapeDtypeStruct(query.shape, jnp.bfloat16),
        compiler_params=pltpu.CompilerParams(vmem_limit_bytes=48 * 1024 * 1024),
        cost_estimate=pl.CostEstimate(
            flops=4 * blocks * rows * width * tokens * 3,
            bytes_accessed=4 * blocks * rows * width + 2 * sum(x.size for x in kv_pieces),
            transcendentals=blocks * rows * (width // HD) * tokens * 3,
        ),
        name="attend",
    )(info, query, *kv_pieces)


def turn_kernel(width, step, x_ref, scale_ref, angle_ref, gain_ref, query_ref, kv_ref):
    def block(b, carry):
        rows = pl.ds(pl.multiple_of(b * step, step), step)
        cosine = angle_ref[rows, :HD]
        sine = angle_ref[rows, HD:]
        for j, out_ref in enumerate((query_ref, kv_ref)):
            scale = scale_ref[rows, j : j + 1]
            for at in range(0, width, HD):
                x = x_ref[rows, j * width + at : j * width + at + HD]
                x = x * scale * gain_ref[j : j + 1, at : at + HD]
                turned = x * cosine + pltpu.roll(x, HD // 2, 1) * sine
                out_ref[rows, at : at + HD] = turned.astype(out_ref.dtype)
        kv_ref[rows, width:] = x_ref[rows, 2 * width :].astype(kv_ref.dtype)
        return carry

    lax.fori_loop(0, x_ref.shape[0] // step, block, 0)


def turn(projected, scales, angles, gain):
    rows, width = projected.shape[0], projected.shape[1] // 3
    whole = pl.BlockSpec(memory_space=pltpu.VMEM)
    return pl.pallas_call(
        functools.partial(turn_kernel, width, 80 if rows % 80 == 0 else rows),
        in_specs=[whole] * 4,
        out_specs=[whole] * 2,
        out_shape=[
            jax.ShapeDtypeStruct((rows, width), jnp.bfloat16),
            jax.ShapeDtypeStruct((rows, 2 * width), jnp.bfloat16),
        ],
        compiler_params=pltpu.CompilerParams(vmem_limit_bytes=32 * 1024 * 1024),
        cost_estimate=pl.CostEstimate(
            flops=10 * rows * width, bytes_accessed=18 * rows * width, transcendentals=0
        ),
        name="turn",
    )(projected, scales, angles, gain)


def page_kernel(info, key_ref, value_ref, out_ref):
    page = info[pl.program_id(0)]
    row = page * PAGE + lax.broadcasted_iota(jnp.int32, (PAGE, 1), 0)
    inside = row < info[PAGES]
    for j, ref in enumerate((key_ref, value_ref)):
        kept = jnp.where(inside, ref[...].astype(jnp.float32), 0.0)
        out_ref[0, j] = kept.astype(out_ref.dtype)


def place_pages(keys, values, info):
    width = keys.shape[1]
    spec = pl.BlockSpec((PAGE, width), lambda s, info: (info[s], 0))
    return pl.pallas_call(
        page_kernel,
        grid_spec=pltpu.PrefetchScalarGridSpec(
            num_scalar_prefetch=1,
            grid=(PAGES,),
            in_specs=[spec, spec],
            out_specs=pl.BlockSpec((1, 2, PAGE, width), lambda s, info: (s, 0, 0, 0)),
        ),
        out_shape=jax.ShapeDtypeStruct((PAGES, 2, PAGE, width), keys.dtype),
        cost_estimate=pl.CostEstimate(
            flops=2 * keys.size, bytes_accessed=8 * keys.size, transcendentals=0
        ),
        name="place_pages",
    )(info, keys, values)


def local(
    hidden, lengths, owner, page_table, qkv_train, qk_gain, o_weight, post_gain, gate_up_train
):
    grid = Grid()
    n_row, n_col, planes = grid.n_row, grid.n_col, grid.planes
    row, col, plane, core = grid.row, grid.col, grid.plane, grid.core
    bf16 = jnp.bfloat16
    prompts = lengths.shape[0]
    tokens, width = hidden.shape
    part = tokens // n_row
    row_width = width // n_row
    col_block = row_width // n_col
    units = qkv_train.shape[2]
    heads_width = units * n_col
    ff_units = gate_up_train.shape[2]

    prompt_ends = jnp.cumsum(lengths)
    prompt_starts = prompt_ends - lengths

    quarter = lax.dynamic_slice_in_dim(hidden, row * part, part, 0).reshape(part, n_row, row_width)
    quarter = jnp.concatenate([pick(quarter, row ^ i, 1) for i in range(n_row)], axis=1)
    gathered = lax.all_gather(quarter, "col", axis=0, tiled=True)
    head_rows = o_weight.shape[0] // 2
    half_rows = lax.dynamic_slice_in_dim(o_weight, core * head_rows, head_rows, 0)
    columns = [
        lax.dynamic_slice_in_dim(half_rows, (row ^ i) * row_width, row_width, 1)
        for i in range(n_row)
    ]
    weights = qkv_train.astype(bf16).transpose(1, 0, 2).reshape(row_width, 3 * units)
    weights, columns, gate_up_train = together(weights, columns, gate_up_train)
    columns = [columns[0]] + [grid.row_xor(columns[i], i) for i in range(1, n_row)]
    gain_halves = halves(qk_gain, row_width // 40, 3 * units)
    weight_pieces = grid.gather_row(jnp.concatenate([weights, gain_halves], axis=0))
    gain = jnp.stack([x[row_width:] for x in weight_pieces])
    weight_pieces = [x[:row_width] for x in weight_pieces]

    def swap_cores(blocks, axis):
        other = grid.other_core(pick(blocks, 1 - core, axis))
        return pick(blocks, core, axis), other

    def ff_blocks(matrix):
        blocks = matrix.astype(bf16).reshape(planes, 2, col_block, ff_units)
        return grid.join_cores(*swap_cores(blocks, 1), 2)

    gate_blocks, own_weights = together(ff_blocks(gate_up_train[0]), weights)
    at_planes_gate = grid.over_planes(gate_blocks)
    qkv_blocks = grid.join_cores(
        *swap_cores(own_weights.reshape(planes, 2, col_block, 3, units), 1), 3
    ).reshape(planes, col_block, 6 * units)
    gathered, qkv_blocks, columns, gain = together(gathered, qkv_blocks, columns, gain)
    columns = jnp.stack(columns)
    columns_other = grid.other_core(columns)
    gain = unhalved(pick(gain, plane ^ row), qk_gain.shape)
    whole_heads = units % HD == 0
    held = units if whole_heads else 2 * units
    if whole_heads:
        gain = lax.dynamic_slice_in_dim(gain, core * units, units, 1)

    projected = jnp.dot(
        gathered, jnp.concatenate(weight_pieces, axis=0), preferred_element_type=jnp.float32
    )
    rows_here = n_col * part
    squares = jnp.stack(
        [
            jnp.sum(jnp.square(projected[:, j * units : (j + 1) * units]), axis=1)
            for j in range(2)
        ]
    )
    squares = jnp.sum(lax.all_gather(squares, "col", axis=0), axis=0)
    squares, at_planes_gate, qkv_blocks = together(squares, at_planes_gate, qkv_blocks)
    at_planes_qkv = grid.over_planes(qkv_blocks)
    inverse = inverse_rms(squares, heads_width).T
    if not whole_heads:
        projected = projected.reshape(rows_here, 3, units)
        projected = grid.join_cores(projected, grid.other_core(projected), 2)
        projected = projected.reshape(rows_here, 3 * held)

    token = (
        jnp.arange(n_col, dtype=jnp.int32)[:, None] * tokens
        + row * part
        + jnp.arange(part, dtype=jnp.int32)[None, :]
    ).reshape(rows_here)
    start = jnp.max(jnp.where(token[:, None] >= prompt_ends[None, :], prompt_ends[None, :], 0), axis=1)
    position = token - start
    half = HD // 2
    frequency = rope_theta ** (-2.0 * jnp.arange(half, dtype=jnp.float32) / HD)
    turns = position.astype(jnp.float32)[:, None] * frequency[None, :]
    cosine, sine = jnp.cos(turns), jnp.sin(turns)
    angles = jnp.concatenate([cosine, cosine, -sine, sine], axis=1)
    query, kv = turn(projected, inverse, angles, gain)

    query, kv, columns_other = together(query, kv, columns_other)
    key_or_value = [
        lax.dynamic_slice_in_dim(kv, j * held + core * units, units, 1)
        if not whole_heads
        else kv[:, j * units : (j + 1) * units]
        for j in range(2)
    ]
    same_core = [list(range(k, n_col, 2)) for k in range(2)]
    key_planes, value_planes = [
        lax.all_gather(x, "col", axis=0, axis_index_groups=same_core) for x in key_or_value
    ]

    kv_pieces = [x.reshape(n_col, part, 2 * held) for x in grid.gather_row(kv)]
    offsets = jnp.stack([(row ^ i) * part for i in range(n_row)])
    if part % 16:
        stacked = jnp.stack(kv_pieces)
        natural = jnp.stack([pick(stacked, row ^ r) for r in range(n_row)], axis=1)
        kv_pieces = [natural.reshape(n_col, tokens, 2 * held)]
        offsets = jnp.zeros((1,), jnp.int32)
    info = jnp.concatenate([prompt_ends, (row * part)[None], offsets]).astype(jnp.int32)
    kv_pieces[-1], at_planes_gate = together(kv_pieces[-1], at_planes_gate)
    at_rows_gate = grid.over_rows(at_planes_gate)
    attention = attend(query.reshape(n_col, part, held), kv_pieces, info, tokens, prompts)

    attention = attention.reshape(planes, 2, part, held)
    mine = pick(attention, core, 1)
    if whole_heads:
        attention = grid.join_cores(mine, grid.other_core(pick(attention, 1 - core, 1)), 2)
    else:
        attention = mine
    attention, key_planes, at_planes_qkv, at_rows_gate, gate_up_train = together(
        attention, key_planes, at_planes_qkv, at_rows_gate, gate_up_train
    )
    arrived = grid.over_planes(attention)
    key_rows = grid.over_rows(key_planes)
    at_rows_qkv = grid.over_rows(at_planes_qkv)
    up_blocks = ff_blocks(gate_up_train[1])
    up_cut = col_block * 4 // 5
    up_blocks, last_blocks = up_blocks[:, :up_cut], up_blocks[:, up_cut:]
    arrived, key_rows, at_rows_qkv, value_planes, up_blocks, last_blocks = together(
        arrived, key_rows, at_rows_qkv, value_planes, up_blocks, last_blocks
    )
    at_planes_up = grid.over_planes(up_blocks)
    value_rows = grid.over_rows(value_planes)
    o_columns = jnp.concatenate(
        [
            grid.join_cores(pick(columns, row ^ r), pick(columns_other, row ^ r), 0)
            for r in range(n_row)
        ],
        axis=0,
    )
    attention = jnp.concatenate(list(arrived), axis=1)
    attention_rows = jnp.concatenate(grid.in_order(grid.gather_row(attention)), axis=0)
    attention_rows, at_planes_up, last_blocks, at_rows_gate = together(
        attention_rows, at_planes_up, last_blocks, at_rows_gate
    )
    at_planes_last = grid.over_planes(last_blocks)
    at_rows_up = grid.over_rows(at_planes_up)
    summed = jnp.dot(attention_rows, o_columns, preferred_element_type=jnp.float32)
    most = PAGES * PAGE

    def start_of(owner_col):
        return jnp.sum(jnp.where(owner == owner_col, prompt_starts, 0))

    def window(rows):
        rows = jnp.stack(rows).reshape(n_row, n_col, part, units).transpose(1, 0, 2, 3)
        rows = rows.reshape(n_col * tokens, units)
        rows = jnp.concatenate([rows, jnp.zeros((most, units), bf16)], axis=0)
        other = grid.other_core(lax.dynamic_slice_in_dim(rows, start_of(col ^ 1), most, 0))
        return grid.join_cores(
            lax.dynamic_slice_in_dim(rows, start_of(col), most, 0), other, 1
        )

    mine = owner == col
    my_length = jnp.sum(jnp.where(mine, lengths, 0))
    my_table = jnp.sum(jnp.where(mine[:, None], page_table, 0), axis=0)
    page_index = jnp.arange(PAGES, dtype=jnp.int32)
    page_of_slot = jnp.sum(
        jnp.where(my_table[None, :] == page_index[:, None], page_index[None, :], 0), axis=1
    )
    page_of_slot = jnp.where(jnp.any(mine), page_of_slot, 0)
    key_window, value_window = window(key_rows), window(value_rows)
    def place_rows(whole, blocks, j, low):
        return lax.dynamic_update_slice(whole, jnp.stack(blocks)[None], (j, 0, low, 0))

    ff_server = jnp.zeros((2, n_row, col_block, 2 * ff_units), bf16)
    ff_server = place_rows(ff_server, at_rows_gate, 0, 0)
    cache = place_pages(
        key_window,
        value_window,
        jnp.concatenate([page_of_slot, my_length[None]]).astype(jnp.int32),
    )
    summed, cache, ff_server = together(summed, cache, ff_server)
    out_squares = lax.psum(jnp.sum(summed * summed, axis=1), "row")
    out_squares, at_planes_last = together(out_squares, at_planes_last)
    ff_server = place_rows(ff_server, at_rows_up, 1, 0)
    ff_server = place_rows(ff_server, grid.over_rows(at_planes_last), 1, up_cut)
    normalized = summed * inverse_rms(out_squares, width)[:, None] * post_gain
    residual = lax.dynamic_slice_in_dim(hidden, row * row_width, row_width, 1).astype(jnp.float32)
    layer_out = (residual + normalized).astype(bf16)

    qkv_server = jnp.stack(at_rows_qkv).reshape(n_row, col_block, 3, 2 * units).transpose(2, 0, 1, 3)
    return (layer_out, cache[None], qkv_server, ff_server)


def solution(mesh):
    in_specs = (
        P("col", None),
        P(),
        P(),
        P(),
        P(None, "row", "col"),
        P(None, "row"),
        P("row", None),
        P("row"),
        P(None, "row", "col"),
    )
    out_specs = (
        P("col", "row"),
        P("col", None, None, None, "row"),
        P(None, None, "col", "row"),
        P(None, None, "col", "row"),
    )
    return jax.shard_map(local, mesh=mesh, in_specs=in_specs, out_specs=out_specs, check_vma=False)
```

```python
import functools
import math

import jax
import jax.numpy as jnp
from jax import lax
from jax.experimental import pallas as pl
from jax.experimental.pallas import tpu as pltpu
from jax.sharding import PartitionSpec as P

HD = 128
PAGE = 128
PAGES = 16
BOTH = ("row", "col")

norm_epsilon = 1e-06
rope_theta = 500000.0
big_negative = -1e30


def inverse_rms(squares, features):
    return lax.rsqrt(squares / features + norm_epsilon)


def permute(x, n_row, n_col, target):
    pairs = []
    for r in range(n_row):
        for c in range(n_col):
            r2, c2 = target(r, c)
            pairs.append((r * n_col + c, r2 * n_col + c2))
    return lax.ppermute(x, BOTH, pairs)


def together(*values):
    return lax.optimization_barrier(values)


def pick(x, index, axis=0):
    return lax.dynamic_index_in_dim(x, index, axis, keepdims=False)


def halves(x, rows, width):
    upper = lax.reduce_precision(x, 8, 7)
    pairs = jnp.stack([upper, x - upper]).astype(jnp.bfloat16).reshape(-1)
    return jnp.pad(pairs, (0, rows * width - pairs.size)).reshape(rows, width)


def unhalved(pairs, shape):
    count = 2 * math.prod(shape)
    pairs = pairs.reshape(-1)[:count].astype(jnp.float32)
    return jnp.sum(pairs.reshape((2,) + tuple(shape)), axis=0)


class Grid:
    def __init__(self):
        self.n_row = lax.axis_size("row")
        self.n_col = lax.axis_size("col")
        self.planes = self.n_col // 2
        self.row = lax.axis_index("row")
        self.col = lax.axis_index("col")
        self.plane = self.col // 2
        self.core = self.col % 2

    def move(self, x, target):
        return permute(x, self.n_row, self.n_col, target)

    def other_core(self, x):
        return self.move(x, lambda r, c: (r, c ^ 1))

    def row_xor(self, x, i):
        return self.move(x, lambda r, c: (r ^ i, c))

    def gather_row(self, x):
        if self.n_row != 4:
            return [x] + [self.row_xor(x, i) for i in range(1, self.n_row)]
        half = x.shape[0] // 2
        first = self.row_xor(x, 1)
        second = self.row_xor(x, 2)
        third = jnp.concatenate(
            [self.row_xor(first[:half], 2), self.row_xor(second[half:], 1)], axis=0
        )
        return [x, first, second, third]

    def over_planes(self, blocks):
        groups = [list(range(k, self.n_col, 2)) for k in range(2)]
        return lax.all_to_all(
            blocks, "col", split_axis=0, concat_axis=0, tiled=True, axis_index_groups=groups
        )

    def over_rows(self, blocks):
        moved = [pick(blocks, self.row)]
        for i in range(1, self.n_row):
            moved.append(self.row_xor(pick(blocks, self.row ^ i), i))
        return self.in_order(moved)

    def in_order(self, moved):
        stacked = jnp.stack(moved)
        return [pick(stacked, r ^ self.row) for r in range(self.n_row)]

    def join_cores(self, mine, other, axis):
        return jnp.where(
            self.core == 0,
            jnp.concatenate([mine, other], axis=axis),
            jnp.concatenate([other, mine], axis=axis),
        )


def attend_kernel(pieces, tokens, piece_tokens, heads, prompts, info, q_ref, *refs):
    kv_refs, out_ref = refs[:pieces], refs[pieces]
    block = pl.program_id(0)
    rows = q_ref.shape[1]
    width = heads * HD
    scale = math.log2(math.e) / math.sqrt(HD)
    first = block * tokens + info[prompts]
    first_start = jnp.int32(0)
    row_id = first + lax.broadcasted_iota(jnp.int32, (rows, 1), 0)
    row_start = jnp.zeros((rows, 1), jnp.int32)
    for p in range(prompts):
        end = info[p]
        first_start = jnp.where(end <= first, jnp.maximum(first_start, end), first_start)
        row_start = jnp.where(end <= row_id, jnp.maximum(row_start, end), row_start)
    lowest = first_start // tokens
    lane = lax.broadcasted_iota(jnp.int32, (1, tokens), 1)
    place = lane + info[prompts + 1]
    for i in range(1, pieces):
        place = jnp.where(
            lane >= i * piece_tokens, lane + (info[prompts + 1 + i] - i * piece_tokens), place
        )
    for head in range(heads):
        at = head * HD
        query = q_ref[0, :, at : at + HD]

        def step(chunk, state):
            top, total, acc = state
            keys = jnp.concatenate([ref[chunk, :, at : at + HD] for ref in kv_refs], axis=0)
            values = jnp.concatenate(
                [ref[chunk, :, width + at : width + at + HD] for ref in kv_refs], axis=0
            )
            scores = lax.dot_general(
                query, keys, (((1,), (1,)), ((), ())), preferred_element_type=jnp.float32
            )
            key_id = chunk * tokens + place
            allowed = (key_id <= row_id) & (key_id >= row_start)
            scores = jnp.where(allowed, scores, big_negative)
            new_top = jnp.maximum(top, jnp.max(scores, axis=1, keepdims=True))
            shrink = jnp.exp2((top - new_top) * scale)
            weights = jnp.exp2((scores - new_top) * scale)
            total = total * shrink + jnp.sum(weights, axis=1, keepdims=True)
            acc = acc * shrink + jnp.dot(
                weights.astype(jnp.bfloat16), values, preferred_element_type=jnp.float32
            )
            return new_top, total, acc

        state = (
            jnp.full((rows, 1), big_negative, jnp.float32),
            jnp.zeros((rows, 1), jnp.float32),
            jnp.zeros((rows, HD), jnp.float32),
        )
        top, total, acc = lax.fori_loop(lowest, block + 1, step, state)
        out_ref[0, :, at : at + HD] = (acc / total).astype(out_ref.dtype)


def attend(query, kv_pieces, info, tokens, prompts):
    blocks, rows, width = query.shape
    pieces = len(kv_pieces)
    piece_tokens = kv_pieces[0].shape[1]
    kernel = functools.partial(
        attend_kernel, pieces, tokens, piece_tokens, width // HD, prompts
    )
    return pl.pallas_call(
        kernel,
        grid_spec=pltpu.PrefetchScalarGridSpec(
            num_scalar_prefetch=1,
            grid=(blocks,),
            in_specs=[pl.BlockSpec((1, rows, width), lambda b, info: (b, 0, 0))]
            + [pl.BlockSpec(x.shape, lambda b, info: (0, 0, 0)) for x in kv_pieces],
            out_specs=pl.BlockSpec((1, rows, width), lambda b, info: (b, 0, 0)),
        ),
        out_shape=jax.ShapeDtypeStruct(query.shape, jnp.bfloat16),
        compiler_params=pltpu.CompilerParams(vmem_limit_bytes=48 * 1024 * 1024),
        cost_estimate=pl.CostEstimate(
            flops=4 * blocks * rows * width * tokens * 3,
            bytes_accessed=4 * blocks * rows * width + 2 * sum(x.size for x in kv_pieces),
            transcendentals=blocks * rows * (width // HD) * tokens * 3,
        ),
        name="attend",
    )(info, query, *kv_pieces)


def turn_kernel(width, step, x_ref, scale_ref, angle_ref, gain_ref, query_ref, kv_ref):
    def block(b, carry):
        rows = pl.ds(pl.multiple_of(b * step, step), step)
        cosine = angle_ref[rows, :HD]
        sine = angle_ref[rows, HD:]
        for j, out_ref in enumerate((query_ref, kv_ref)):
            scale = scale_ref[rows, j : j + 1]
            for at in range(0, width, HD):
                x = x_ref[rows, j * width + at : j * width + at + HD]
                x = x * scale * gain_ref[j : j + 1, at : at + HD]
                turned = x * cosine + pltpu.roll(x, HD // 2, 1) * sine
                out_ref[rows, at : at + HD] = turned.astype(out_ref.dtype)
        kv_ref[rows, width:] = x_ref[rows, 2 * width :].astype(kv_ref.dtype)
        return carry

    lax.fori_loop(0, x_ref.shape[0] // step, block, 0)


def turn(projected, scales, angles, gain):
    rows, width = projected.shape[0], projected.shape[1] // 3
    whole = pl.BlockSpec(memory_space=pltpu.VMEM)
    return pl.pallas_call(
        functools.partial(turn_kernel, width, 80 if rows % 80 == 0 else rows),
        in_specs=[whole] * 4,
        out_specs=[whole] * 2,
        out_shape=[
            jax.ShapeDtypeStruct((rows, width), jnp.bfloat16),
            jax.ShapeDtypeStruct((rows, 2 * width), jnp.bfloat16),
        ],
        compiler_params=pltpu.CompilerParams(vmem_limit_bytes=32 * 1024 * 1024),
        cost_estimate=pl.CostEstimate(
            flops=10 * rows * width, bytes_accessed=18 * rows * width, transcendentals=0
        ),
        name="turn",
    )(projected, scales, angles, gain)


def page_kernel(info, key_ref, value_ref, out_ref):
    page = info[pl.program_id(0)]
    row = page * PAGE + lax.broadcasted_iota(jnp.int32, (PAGE, 1), 0)
    inside = row < info[PAGES]
    for j, ref in enumerate((key_ref, value_ref)):
        kept = jnp.where(inside, ref[...].astype(jnp.float32), 0.0)
        out_ref[0, j] = kept.astype(out_ref.dtype)


def place_pages(keys, values, info):
    width = keys.shape[1]
    spec = pl.BlockSpec((PAGE, width), lambda s, info: (info[s], 0))
    return pl.pallas_call(
        page_kernel,
        grid_spec=pltpu.PrefetchScalarGridSpec(
            num_scalar_prefetch=1,
            grid=(PAGES,),
            in_specs=[spec, spec],
            out_specs=pl.BlockSpec((1, 2, PAGE, width), lambda s, info: (s, 0, 0, 0)),
        ),
        out_shape=jax.ShapeDtypeStruct((PAGES, 2, PAGE, width), keys.dtype),
        cost_estimate=pl.CostEstimate(
            flops=2 * keys.size, bytes_accessed=8 * keys.size, transcendentals=0
        ),
        name="place_pages",
    )(info, keys, values)


def local(
    hidden, lengths, owner, page_table, qkv_train, qk_gain, o_weight, post_gain, gate_up_train
):
    grid = Grid()
    n_row, n_col, planes = grid.n_row, grid.n_col, grid.planes
    row, col, plane, core = grid.row, grid.col, grid.plane, grid.core
    bf16 = jnp.bfloat16
    prompts = lengths.shape[0]
    tokens, width = hidden.shape
    part = tokens // n_row
    row_width = width // n_row
    col_block = row_width // n_col
    units = qkv_train.shape[2]
    heads_width = units * n_col
    ff_units = gate_up_train.shape[2]

    prompt_ends = jnp.cumsum(lengths)
    prompt_starts = prompt_ends - lengths

    quarter = lax.dynamic_slice_in_dim(hidden, row * part, part, 0).reshape(part, n_row, row_width)
    quarter = jnp.concatenate([pick(quarter, row ^ i, 1) for i in range(n_row)], axis=1)
    gathered = lax.all_gather(quarter, "col", axis=0, tiled=True)
    head_rows = o_weight.shape[0] // 2
    half_rows = lax.dynamic_slice_in_dim(o_weight, core * head_rows, head_rows, 0)
    columns = [
        lax.dynamic_slice_in_dim(half_rows, (row ^ i) * row_width, row_width, 1)
        for i in range(n_row)
    ]
    weights = qkv_train.astype(bf16).transpose(1, 0, 2).reshape(row_width, 3 * units)
    weights, columns, gate_up_train = together(weights, columns, gate_up_train)
    columns = [columns[0]] + [grid.row_xor(columns[i], i) for i in range(1, n_row)]
    gain_halves = halves(qk_gain, row_width // 40, 3 * units)
    weight_pieces = grid.gather_row(jnp.concatenate([weights, gain_halves], axis=0))
    gain = jnp.stack([x[row_width:] for x in weight_pieces])
    weight_pieces = [x[:row_width] for x in weight_pieces]

    def swap_cores(blocks, axis):
        other = grid.other_core(pick(blocks, 1 - core, axis))
        return pick(blocks, core, axis), other

    def ff_blocks(matrix):
        blocks = matrix.astype(bf16).reshape(planes, 2, col_block, ff_units)
        return grid.join_cores(*swap_cores(blocks, 1), 2)

    gate_blocks, own_weights = together(ff_blocks(gate_up_train[0]), weights)
    at_planes_gate = grid.over_planes(gate_blocks)
    qkv_blocks = grid.join_cores(
        *swap_cores(own_weights.reshape(planes, 2, col_block, 3, units), 1), 3
    ).reshape(planes, col_block, 6 * units)
    gathered, qkv_blocks, columns, gain = together(gathered, qkv_blocks, columns, gain)
    columns = jnp.stack(columns)
    columns_other = grid.other_core(columns)
    gain = unhalved(pick(gain, plane ^ row), qk_gain.shape)
    whole_heads = units % HD == 0
    held = units if whole_heads else 2 * units
    if whole_heads:
        gain = lax.dynamic_slice_in_dim(gain, core * units, units, 1)

    projected = jnp.dot(
        gathered, jnp.concatenate(weight_pieces, axis=0), preferred_element_type=jnp.float32
    )
    rows_here = n_col * part
    squares = jnp.stack(
        [
            jnp.sum(jnp.square(projected[:, j * units : (j + 1) * units]), axis=1)
            for j in range(2)
        ]
    )
    squares = jnp.sum(lax.all_gather(squares, "col", axis=0), axis=0)
    squares, at_planes_gate, qkv_blocks = together(squares, at_planes_gate, qkv_blocks)
    at_planes_qkv = grid.over_planes(qkv_blocks)
    inverse = inverse_rms(squares, heads_width).T
    if not whole_heads:
        projected = projected.reshape(rows_here, 3, units)
        projected = grid.join_cores(projected, grid.other_core(projected), 2)
        projected = projected.reshape(rows_here, 3 * held)

    token = (
        jnp.arange(n_col, dtype=jnp.int32)[:, None] * tokens
        + row * part
        + jnp.arange(part, dtype=jnp.int32)[None, :]
    ).reshape(rows_here)
    start = jnp.max(jnp.where(token[:, None] >= prompt_ends[None, :], prompt_ends[None, :], 0), axis=1)
    position = token - start
    half = HD // 2
    frequency = rope_theta ** (-2.0 * jnp.arange(half, dtype=jnp.float32) / HD)
    turns = position.astype(jnp.float32)[:, None] * frequency[None, :]
    cosine, sine = jnp.cos(turns), jnp.sin(turns)
    angles = jnp.concatenate([cosine, cosine, -sine, sine], axis=1)
    query, kv = turn(projected, inverse, angles, gain)

    query, kv, columns_other = together(query, kv, columns_other)
    key_or_value = [
        lax.dynamic_slice_in_dim(kv, j * held + core * units, units, 1)
        if not whole_heads
        else kv[:, j * units : (j + 1) * units]
        for j in range(2)
    ]
    same_core = [list(range(k, n_col, 2)) for k in range(2)]
    key_planes, value_planes = [
        lax.all_gather(x, "col", axis=0, axis_index_groups=same_core) for x in key_or_value
    ]

    kv_pieces = [x.reshape(n_col, part, 2 * held) for x in grid.gather_row(kv)]
    offsets = jnp.stack([(row ^ i) * part for i in range(n_row)])
    if part % 16:
        stacked = jnp.stack(kv_pieces)
        natural = jnp.stack([pick(stacked, row ^ r) for r in range(n_row)], axis=1)
        kv_pieces = [natural.reshape(n_col, tokens, 2 * held)]
        offsets = jnp.zeros((1,), jnp.int32)
    info = jnp.concatenate([prompt_ends, (row * part)[None], offsets]).astype(jnp.int32)
    kv_pieces[-1], at_planes_gate = together(kv_pieces[-1], at_planes_gate)
    at_rows_gate = grid.over_rows(at_planes_gate)
    attention = attend(query.reshape(n_col, part, held), kv_pieces, info, tokens, prompts)

    attention = attention.reshape(planes, 2, part, held)
    mine = pick(attention, core, 1)
    if whole_heads:
        attention = grid.join_cores(mine, grid.other_core(pick(attention, 1 - core, 1)), 2)
    else:
        attention = mine
    attention, key_planes, at_planes_qkv, at_rows_gate, gate_up_train = together(
        attention, key_planes, at_planes_qkv, at_rows_gate, gate_up_train
    )
    arrived = grid.over_planes(attention)
    key_rows = grid.over_rows(key_planes)
    at_rows_qkv = grid.over_rows(at_planes_qkv)
    up_blocks = ff_blocks(gate_up_train[1])
    up_cut = col_block * 4 // 5
    up_blocks, last_blocks = up_blocks[:, :up_cut], up_blocks[:, up_cut:]
    arrived, key_rows, at_rows_qkv, value_planes, up_blocks, last_blocks = together(
        arrived, key_rows, at_rows_qkv, value_planes, up_blocks, last_blocks
    )
    at_planes_up = grid.over_planes(up_blocks)
    value_rows = grid.over_rows(value_planes)
    o_columns = jnp.concatenate(
        [
            grid.join_cores(pick(columns, row ^ r), pick(columns_other, row ^ r), 0)
            for r in range(n_row)
        ],
        axis=0,
    )
    attention = jnp.concatenate(list(arrived), axis=1)
    attention_rows = jnp.concatenate(grid.in_order(grid.gather_row(attention)), axis=0)
    most = PAGES * PAGE

    def start_of(owner_col):
        return jnp.sum(jnp.where(owner == owner_col, prompt_starts, 0))

    def window(rows):
        rows = jnp.stack(rows).reshape(n_row, n_col, part, units).transpose(1, 0, 2, 3)
        rows = rows.reshape(n_col * tokens, units)
        rows = jnp.concatenate([rows, jnp.zeros((most, units), bf16)], axis=0)
        other = grid.other_core(lax.dynamic_slice_in_dim(rows, start_of(col ^ 1), most, 0))
        return grid.join_cores(
            lax.dynamic_slice_in_dim(rows, start_of(col), most, 0), other, 1
        )

    mine = owner == col
    my_length = jnp.sum(jnp.where(mine, lengths, 0))
    my_table = jnp.sum(jnp.where(mine[:, None], page_table, 0), axis=0)
    page_index = jnp.arange(PAGES, dtype=jnp.int32)
    page_of_slot = jnp.sum(
        jnp.where(my_table[None, :] == page_index[:, None], page_index[None, :], 0), axis=1
    )
    page_of_slot = jnp.where(jnp.any(mine), page_of_slot, 0)
    key_window, value_window = window(key_rows), window(value_rows)
    attention_rows, at_planes_up, last_blocks, at_rows_gate, key_window, value_window = together(
        attention_rows, at_planes_up, last_blocks, at_rows_gate, key_window, value_window
    )
    at_planes_last = grid.over_planes(last_blocks)
    at_rows_up = grid.over_rows(at_planes_up)
    summed = jnp.dot(attention_rows, o_columns, preferred_element_type=jnp.float32)
    def place_rows(whole, blocks, j, low):
        return lax.dynamic_update_slice(whole, jnp.stack(blocks)[None], (j, 0, low, 0))

    ff_server = jnp.zeros((2, n_row, col_block, 2 * ff_units), bf16)
    ff_server = place_rows(ff_server, at_rows_gate, 0, 0)
    cache = place_pages(
        key_window,
        value_window,
        jnp.concatenate([page_of_slot, my_length[None]]).astype(jnp.int32),
    )
    summed, cache, ff_server = together(summed, cache, ff_server)
    out_squares = lax.psum(jnp.sum(summed * summed, axis=1), "row")
    out_squares, at_planes_last = together(out_squares, at_planes_last)
    ff_server = place_rows(ff_server, at_rows_up, 1, 0)
    ff_server = place_rows(ff_server, grid.over_rows(at_planes_last), 1, up_cut)
    normalized = summed * inverse_rms(out_squares, width)[:, None] * post_gain
    residual = lax.dynamic_slice_in_dim(hidden, row * row_width, row_width, 1).astype(jnp.float32)
    layer_out = (residual + normalized).astype(bf16)

    qkv_server = jnp.stack(at_rows_qkv).reshape(n_row, col_block, 3, 2 * units).transpose(2, 0, 1, 3)
    return (layer_out, cache[None], qkv_server, ff_server)


def solution(mesh):
    in_specs = (
        P("col", None),
        P(),
        P(),
        P(),
        P(None, "row", "col"),
        P(None, "row"),
        P("row", None),
        P("row"),
        P(None, "row", "col"),
    )
    out_specs = (
        P("col", "row"),
        P("col", None, None, None, "row"),
        P(None, None, "col", "row"),
        P(None, None, "col", "row"),
    )
    return jax.shard_map(local, mesh=mesh, in_specs=in_specs, out_specs=out_specs, check_vma=False)
```
